256 devices in a mesh: row: 8 (over x, z_hi), col: 32 (over z_lo, y, core).
Axes of the slice: x: 4, y: 4, z: 8 (z_hi: 2, z_lo: 4; z = z_hi * 4 + z_lo), core: 2. Of those that a mesh axis runs over, the one named last changes fastest.
Arguments:
- inputs: bfloat16 [512, 8192], P('col', 'row'), may hold values from -6 to 6
- out_grad: bfloat16 [512, 8192], P('col', 'row'), may hold values from -1.5 to 1.5
- gate_weight: bfloat16 [8192, 28672], P('row', 'col'), may hold values from -0.0625 to 0.0625
- up_weight: bfloat16 [8192, 28672], P('row', 'col'), may hold values from -0.0625 to 0.0625
- down_weight: bfloat16 [28672, 8192], P('col', 'row'), may hold values from -0.03125 to 0.03125
Outputs:
- input_grad: bfloat16 [512, 8192], P('col', 'row')
- gate_weight_grad: bfloat16 [8192, 28672], P('row', 'col')
- up_weight_grad: bfloat16 [8192, 28672], P('row', 'col')
- down_weight_grad: bfloat16 [28672, 8192], P('col', 'row')
The draws below stay inside these ranges and needn't reach their ends.
All inputs are finite; a program needn't handle non-finite values.
Results may differ from the reference program's by a relative error of at most 0.005.
Values may be sent and summed in bfloat16 or wider, within the bound.
A program may use at most 64 MiB of HBM per device.

```python
import jax
import jax.numpy as jnp

D = 8192
FF = 28672
TOKENS = 512


def spiked(drawn, rng, source, target, parts, factor):
    def block_of(axis_at):
        return (jnp.arange(drawn.shape[axis_at]) // (drawn.shape[axis_at] // parts)).reshape((-1,) + (1,) * (drawn.ndim - 1 - axis_at))

    one_side = jax.random.permutation(rng, parts)[block_of(target)]
    other_side = (block_of(target) + parts // 2) % parts
    return jnp.where((block_of(source) == one_side) | (block_of(source) == other_side), factor * drawn, drawn)


def block_scale(stream_key, dims, cuts, least, high):
    def one(dim, blocks):
        steps = jax.random.uniform(jax.random.fold_in(jax.random.fold_in(stream_key, 6), dim), (blocks,), jnp.float32, least / len(cuts), high / len(cuts))
        return jnp.repeat(jnp.exp(steps), dims[dim] // blocks).reshape((-1,) + (1,) * (len(dims) - dim - 1))

    loudness = one(*cuts[0])
    for cut in cuts[1:]:
        loudness = loudness * one(*cut)
    return loudness


def scatter_about(rng, shape, scale, reach, shards=(), held_as=jnp.bfloat16):
    entries = jax.random.normal(rng, shape, jnp.float32) * scale
    if len(shards) > 0:
        entries = block_scale(rng, shape, shards, -0.22, 0.18) * entries
    return jnp.clip(entries, min=-reach, max=reach).astype(held_as)


def noise_with(stream_key, dims, width, reach, shards, heavy, held_as=jnp.bfloat16):
    entries = width * jax.random.normal(stream_key, dims, jnp.float32)
    if shards:
        entries = entries * block_scale(stream_key, dims, shards, -0.22, 0.18)
    return jnp.clip(spiked(entries, jax.random.fold_in(stream_key, 3), *heavy), -reach, reach).astype(held_as)


def setup_inputs(seed: int = 0) -> dict:
    streams_of = jax.random.split(jax.random.key(seed), 6)
    inputs = noise_with(streams_of[0], (TOKENS, D), 1.0, 6.0, ((0, 32), (1, 8)), (1, 0, 32, 2.75))
    out_grad = noise_with(streams_of[1], (TOKENS, D), 0.25, 1.5, ((0, 32), (1, 8)), (1, 0, 32, 2.75))
    gate_weight = scatter_about(streams_of[2], (D, FF), D ** -0.5, 0.0625, ((0, 8), (1, 32)))
    up_weight = scatter_about(streams_of[3], (D, FF), D ** -0.5, 0.0625, ((0, 8), (1, 32)))
    down_weight = scatter_about(streams_of[4], (FF, D), FF ** -0.5, 0.03125, ((0, 32), (1, 8)))
    return {"inputs": inputs, "out_grad": out_grad, "gate_weight": gate_weight, "up_weight": up_weight, "down_weight": down_weight}


def reference(inputs, out_grad, gate_weight, up_weight, down_weight):
    gate = jnp.dot(inputs, gate_weight, preferred_element_type=jnp.float32)
    up = jnp.dot(inputs, up_weight, preferred_element_type=jnp.float32)
    hidden_grad = jnp.dot(out_grad, down_weight.T, preferred_element_type=jnp.float32)
    sigm = jax.nn.sigmoid(gate)
    act = gate * sigm
    hidden = (act * up).astype(jnp.bfloat16)
    up_grad = (hidden_grad * act).astype(jnp.bfloat16)
    gate_grad = (hidden_grad * up * sigm * (1.0 + gate * (1.0 - sigm))).astype(jnp.bfloat16)
    down_weight_grad = jnp.dot(hidden.T, out_grad, preferred_element_type=jnp.float32).astype(jnp.bfloat16)
    gate_weight_grad = jnp.dot(inputs.T, gate_grad, preferred_element_type=jnp.float32).astype(jnp.bfloat16)
    up_weight_grad = jnp.dot(inputs.T, up_grad, preferred_element_type=jnp.float32).astype(jnp.bfloat16)
    input_grad = (jnp.dot(gate_grad, gate_weight.T, preferred_element_type=jnp.float32)
                  + jnp.dot(up_grad, up_weight.T, preferred_element_type=jnp.float32)).astype(jnp.bfloat16)
    return input_grad, gate_weight_grad, up_weight_grad, down_weight_grad
```

```python
import jax
import jax.numpy as jnp
from jax import lax
from jax.experimental import pallas as pl
from jax.experimental.pallas import tpu as pltpu
from jax.sharding import PartitionSpec as P

MESH = pl.DeviceIdType.MESH
BF16 = jnp.bfloat16
F32 = jnp.float32

CHUNKS = 8
CHUNK_OF = ((0, 0), (1, 0), (3, 0), (1, 1), (3, 1), (2, 0), (2, 1), (0, 1))
LAG_B, LAG_C, LAG_D, LAG_F, LAG_G, LAG_H = 1, 2, 5, 6, 7, 8

RELAY_LO, RELAY_HI, DIRECT_HI, DIRECT_LO, SUM_LO, SUM_HI, ZSUM = range(7)
OWN_UP_LO, OWN_UP_HI, OWN_DN_HI, OWN_DN_LO, FWD_LO, FWD_HI = range(7, 13)
PER_CHUNK = 13
NT = (((1,), (1,)), ((), ()))


def comm_kernel(
    x_hbm, dy_hbm, wg_hbm, wu_hbm, wd_hbm,
    ig_ref, xo_hbm, do_hbm, h_hbm, gg_hbm, ug_hbm,
    xd, wg, wu, wd, part, s_far, s_near, s_sum, s_z, r_relay, r_near, r_sum, r_z, grads,
    ig_part, ig_sib, ig_ysend, ig_yrecv, ig_msend, ig_mrecv, ig_zsend, ig_zrecv,
    load_sem, send, recv, p1_send, p1_recv, sib_send, sib_recv, y_send, y_recv,
    ig_sib_send, ig_sib_recv, ig_y_send, ig_y_recv, ig_z_send, ig_z_recv, out_sem,
):
    ff = wg.shape[1]
    width = 3 * ff
    cut = (width // 256) * 128
    lo, hi = pl.ds(0, cut), pl.ds(cut, width - cut)

    row, col = lax.axis_index("row"), lax.axis_index("col")
    x, zh = row // 2, row % 2
    zl, y, k = col // 8, (col // 2) % 4, col % 2
    zlo = zl % 2

    def dev(x=x, zh=zh, zl=zl, y=y, k=k):
        return (x * 2 + zh, zl * 8 + y * 2 + k)

    xp, xm, xf = (x + 1) % 4, (x + 3) % 4, (x + 2) % 4
    up, down = dev(x=xp), dev(x=xm)
    partner = dev(zh=1 - zh)
    yp, ym, yf = dev(y=(y + 1) % 4), dev(y=(y + 3) % 4), dev(y=(y + 2) % 4)
    mate_z = zl + 1 - 2 * zlo
    mate, other_same, other_diff = dev(zl=mate_z), dev(zl=(zl + 2) % 4), dev(zl=(mate_z + 2) % 4)
    sibling = dev(k=1 - k)

    def remote(src, dst, ssem, rsem, target):
        return pltpu.make_async_remote_copy(
            src_ref=src, dst_ref=dst, send_sem=ssem, recv_sem=rsem, device_id=target, device_id_type=MESH
        )

    loads = [
        pltpu.make_async_copy(x_hbm, xd.at[0, k, zlo, 0], load_sem.at[0]),
        pltpu.make_async_copy(dy_hbm, xd.at[0, k, zlo, 1], load_sem.at[1]),
        pltpu.make_async_copy(wg_hbm, wg, load_sem.at[2]),
        pltpu.make_async_copy(wu_hbm, wu, load_sem.at[3]),
        pltpu.make_async_copy(wd_hbm, wd, load_sem.at[4]),
    ]
    for load in loads:
        load.start()

    barrier = pltpu.get_barrier_semaphore()
    others = (up, down, partner, yp, ym, yf, mate, other_same, other_diff, sibling)
    for other in others:
        pl.semaphore_signal(barrier, inc=1, device_id=other, device_id_type=MESH)
    loads[0].wait()
    loads[1].wait()
    pl.semaphore_wait(barrier, len(others))

    mine = xd.at[0, k, zlo]
    z_gather = [
        remote(mine, xd.at[0, k, zlo], p1_send.at[0], p1_recv.at[0], mate),
        remote(mine, xd.at[7, k, zlo], p1_send.at[1], p1_recv.at[1], other_same),
        remote(mine, xd.at[7, k, zlo], p1_send.at[2], p1_recv.at[2], other_diff),
    ]

    def to_sibling(c):
        return remote(xd.at[c, k], xd.at[c, k], sib_send.at[c], sib_recv.at[c], sibling)

    y_gather = [
        remote(xd.at[0, k], xd.at[2, k], y_send.at[0], y_recv.at[0], yp),
        remote(xd.at[0, k], xd.at[1, k], y_send.at[1], y_recv.at[1], ym),
        remote(xd.at[7, k], xd.at[4, k], y_send.at[2], y_recv.at[2], yp),
        remote(xd.at[7, k], xd.at[3, k], y_send.at[3], y_recv.at[3], ym),
        remote(xd.at[2, k, 0], xd.at[5, k, 0], y_send.at[4], y_recv.at[4], yp),
        remote(xd.at[1, k, 1], xd.at[5, k, 1], y_send.at[5], y_recv.at[5], ym),
        remote(xd.at[4, k, 0], xd.at[6, k, 0], y_send.at[6], y_recv.at[6], yp),
        remote(xd.at[3, k, 1], xd.at[6, k, 1], y_send.at[7], y_recv.at[7], ym),
    ]

    def gather_step(step):
        if step == 0:
            z_gather[0].wait_recv()
            y_gather[0].start()
            y_gather[1].start()
            to_sibling(0).start()
        elif step == 1:
            z_gather[1].wait_recv()
            z_gather[2].wait_recv()
            y_gather[2].start()
            y_gather[3].start()
            to_sibling(7).start()
        elif step == 2:
            y_gather[0].wait_recv()
            y_gather[1].wait_recv()
            y_gather[4].start()
            y_gather[5].start()
            to_sibling(1).start()
            to_sibling(2).start()
        elif step == 3:
            y_gather[2].wait_recv()
            y_gather[3].wait_recv()
            y_gather[6].start()
            y_gather[7].start()
            to_sibling(3).start()
            to_sibling(4).start()
        elif step == 4:
            y_gather[4].wait_recv()
            y_gather[5].wait_recv()
            to_sibling(5).start()
        elif step == 5:
            y_gather[6].wait_recv()
            y_gather[7].wait_recv()
            to_sibling(6).start()

    def copy(c, which):
        ends = {
            RELAY_LO: (s_far.at[c, :, lo], r_relay.at[c, :, lo], up),
            RELAY_HI: (s_far.at[c, :, hi], r_relay.at[c, :, hi], down),
            DIRECT_HI: (s_near.at[c, :, hi], r_near.at[c, :, hi], up),
            DIRECT_LO: (s_near.at[c, :, lo], r_near.at[c, :, lo], down),
            SUM_LO: (s_sum.at[c, :, lo], r_sum.at[c, :, lo], up),
            SUM_HI: (s_sum.at[c, :, hi], r_sum.at[c, :, hi], down),
            ZSUM: (s_z.at[c], r_z.at[c], partner),
            OWN_UP_LO: (grads.at[c, x, :, lo], grads.at[c, x, :, lo], up),
            OWN_UP_HI: (grads.at[c, x, :, hi], grads.at[c, x, :, hi], up),
            OWN_DN_HI: (grads.at[c, x, :, hi], grads.at[c, x, :, hi], down),
            OWN_DN_LO: (grads.at[c, x, :, lo], grads.at[c, x, :, lo], down),
            FWD_LO: (grads.at[c, xm, :, lo], grads.at[c, xm, :, lo], up),
            FWD_HI: (grads.at[c, xp, :, hi], grads.at[c, xp, :, hi], down),
        }
        src, dst, target = ends[which]
        return remote(src, dst, send.at[c, which], recv.at[c, which], target)

    def stage_a(c):
        to_sibling(c).wait_recv()
        xs = xd[c, :, :, 0].reshape(64, -1)
        ds = xd[c, :, :, 1].reshape(64, -1)
        gate = jnp.dot(xs, wg[...], preferred_element_type=F32)
        part[c, :, :, 0:ff] = gate.reshape(4, 16, ff)
        upper = jnp.dot(xs, wu[...], preferred_element_type=F32)
        part[c, :, :, ff : 2 * ff] = upper.reshape(4, 16, ff)
        hgrad = lax.dot_general(ds, wd[...], NT, preferred_element_type=F32)
        part[c, :, :, 2 * ff :] = hgrad.reshape(4, 16, ff)
        s_far[c] = part[c, xf].astype(BF16)
        copy(c, RELAY_LO).start()
        copy(c, RELAY_HI).start()
        s_near[c, :, hi] = part[c, xp, :, hi].astype(BF16)
        s_near[c, :, lo] = part[c, xm, :, lo].astype(BF16)
        copy(c, DIRECT_HI).start()
        copy(c, DIRECT_LO).start()

    def stage_b(c):
        copy(c, RELAY_LO).wait_recv()
        s_sum[c, :, lo] = (part[c, xp, :, lo] + r_relay[c, :, lo].astype(F32)).astype(BF16)
        copy(c, SUM_LO).start()
        copy(c, RELAY_HI).wait_recv()
        s_sum[c, :, hi] = (part[c, xm, :, hi] + r_relay[c, :, hi].astype(F32)).astype(BF16)
        copy(c, SUM_HI).start()

    def stage_c(c):
        for which in (DIRECT_HI, DIRECT_LO, SUM_LO, SUM_HI):
            copy(c, which).wait_recv()
        total = part[c, x] + r_near[c].astype(F32) + r_sum[c].astype(F32)
        part[c, x] = total
        s_z[c] = total.astype(BF16)
        copy(c, ZSUM).start()

    def stage_d(c):
        copy(c, ZSUM).wait_recv()
        gate = part[c, x, :, 0:ff] + r_z[c, :, 0:ff].astype(F32)
        upper = part[c, x, :, ff : 2 * ff] + r_z[c, :, ff : 2 * ff].astype(F32)
        hgrad = part[c, x, :, 2 * ff :] + r_z[c, :, 2 * ff :].astype(F32)
        sigm = 1.0 / (1.0 + jnp.exp(-gate))
        act = gate * sigm
        grads[c, x, :, 0:ff] = (act * upper).astype(BF16)
        grads[c, x, :, ff : 2 * ff] = (hgrad * upper * sigm * (1.0 + gate * (1.0 - sigm))).astype(BF16)
        grads[c, x, :, 2 * ff :] = (hgrad * act).astype(BF16)
        for which in (OWN_UP_LO, OWN_DN_HI, OWN_UP_HI, OWN_DN_LO):
            copy(c, which).start()

    def stage_f(c):
        copy(c, OWN_UP_LO).wait_recv()
        copy(c, FWD_LO).start()
        copy(c, OWN_DN_HI).wait_recv()
        copy(c, FWD_HI).start()

    def outs(c):
        return [
            pltpu.make_async_copy(grads.at[c, :, :, pl.ds(0, ff)], h_hbm.at[c], out_sem.at[c, 0]),
            pltpu.make_async_copy(grads.at[c, :, :, pl.ds(ff, ff)], gg_hbm.at[c], out_sem.at[c, 1]),
            pltpu.make_async_copy(grads.at[c, :, :, pl.ds(2 * ff, ff)], ug_hbm.at[c], out_sem.at[c, 2]),
            pltpu.make_async_copy(xd.at[c, :, :, 0], xo_hbm.at[c], out_sem.at[c, 3]),
            pltpu.make_async_copy(xd.at[c, :, :, 1], do_hbm.at[c], out_sem.at[c, 4]),
        ]

    def ig_to_sibling(c):
        return remote(ig_part.at[c, 1 - k], ig_sib.at[c], ig_sib_send.at[c], ig_sib_recv.at[c], sibling)

    def stage_g(c):
        for which in (OWN_UP_HI, OWN_DN_LO, FWD_LO, FWD_HI):
            copy(c, which).wait_recv()
        for out in outs(c):
            out.start()
        gg = grads[c, :, :, ff : 2 * ff].reshape(64, ff)
        ug = grads[c, :, :, 2 * ff :].reshape(64, ff)
        total = lax.dot_general(gg, wg[...], NT, preferred_element_type=F32)
        total = total + lax.dot_general(ug, wu[...], NT, preferred_element_type=F32)
        ig_part[c] = total.reshape(2, 2, 16, -1)
        ig_to_sibling(c).start()

    def ig_to_y(c):
        dy, other = CHUNK_OF[c]
        slot = (dy - 1) * 2 + other
        target = {1: yp, 2: yf, 3: ym}[dy]
        return remote(ig_ysend.at[slot], ig_yrecv.at[slot], ig_y_send.at[slot], ig_y_recv.at[slot], target)

    def stage_h(c):
        ig_to_sibling(c).wait_recv()
        total = ig_part[c, k] + ig_sib[c]
        ig_part[c, k] = total
        for i in range(1, 7):
            dy, other = CHUNK_OF[i]

            @pl.when(c == i)
            def _(i=i, slot=(dy - 1) * 2 + other):
                ig_ysend[slot] = total
                ig_to_y(i).start()

    def own(other, block):
        total = ig_part[7 * other, k, block]
        for dy in range(3):
            total = total + ig_yrecv[dy * 2 + other, block]
        return total

    to_mate = remote(ig_msend, ig_mrecv, ig_z_send.at[2], ig_z_recv.at[2], mate)

    def send_to_mate():
        for i in (1, 2, 5):
            ig_to_y(i).wait_recv()
        ig_msend[...] = own(0, 1 - zlo)
        to_mate.start()

    for z_copy in z_gather:
        z_copy.start()
    for load in loads[2:]:
        load.wait()

    @pl.loop(0, CHUNKS + LAG_H)
    def _(s):
        for step in range(6):
            at = 0 if step == 0 else step - 1

            def run(step=step):
                gather_step(step)

            if step == 1:
                continue
            pl.when(s == at)(run)

        @pl.when(s < CHUNKS)
        def _():
            stage_a(s)

        @pl.when(s == 0)
        def _():
            gather_step(1)

        pl.when(s == CHUNKS + LAG_H - 1)(send_to_mate)

        for stage, lag in (
            (stage_b, LAG_B), (stage_c, LAG_C), (stage_d, LAG_D), (stage_f, LAG_F), (stage_g, LAG_G), (stage_h, LAG_H),
        ):

            @pl.when((s >= lag) & (s < CHUNKS + lag))
            def _(stage=stage, lag=lag):
                stage(s - lag)

    for i in (3, 4, 6):
        ig_to_y(i).wait_recv()
    z_scatter = []
    for i, (block, target) in enumerate(((zlo, other_same), (1 - zlo, other_diff))):
        ig_zsend[i] = own(1, block).astype(BF16)
        z_copy = remote(ig_zsend.at[i], ig_zrecv.at[i], ig_z_send.at[i], ig_z_recv.at[i], target)
        z_copy.start()
        z_scatter.append(z_copy)
    to_mate.wait_recv()
    total = own(0, zlo) + ig_mrecv[...]
    for i in range(2):
        z_scatter[i].wait_recv()
        total = total + ig_zrecv[i].astype(F32)
    ig_ref[...] = total.astype(BF16)

    for z_copy in z_gather + z_scatter + y_gather + [to_mate]:
        z_copy.wait_send()
    for i in range(1, 7):
        ig_to_y(i).wait_send()

    @pl.loop(0, CHUNKS)
    def _(c):
        for which in range(PER_CHUNK):
            copy(c, which).wait_send()
        to_sibling(c).wait_send()
        ig_to_sibling(c).wait_send()
        for out in outs(c):
            out.wait()


def body(inputs, out_grad, gate_weight, up_weight, down_weight):
    feats, ff = gate_weight.shape
    blocks = (CHUNKS, 4, 16)
    anywhere = pl.BlockSpec(memory_space=pl.ANY)
    slot = (CHUNKS, 16, 3 * ff)
    dma = pltpu.SemaphoreType.DMA
    input_grad, x_all, d_all, hidden, gate_grad, up_grad = pl.pallas_call(
        comm_kernel,
        out_shape=[
            jax.ShapeDtypeStruct((16, feats), BF16),
            jax.ShapeDtypeStruct((CHUNKS, 2, 2, 16, feats), BF16),
            jax.ShapeDtypeStruct((CHUNKS, 2, 2, 16, feats), BF16),
            jax.ShapeDtypeStruct(blocks + (ff,), BF16),
            jax.ShapeDtypeStruct(blocks + (ff,), BF16),
            jax.ShapeDtypeStruct(blocks + (ff,), BF16),
        ],
        in_specs=[anywhere] * 5,
        out_specs=[pl.BlockSpec(memory_space=pltpu.VMEM)] + [anywhere] * 5,
        scratch_shapes=[
            pltpu.VMEM((CHUNKS, 2, 2, 2, 16, feats), BF16),
            pltpu.VMEM((feats, ff), BF16),
            pltpu.VMEM((feats, ff), BF16),
            pltpu.VMEM((ff, feats), BF16),
            pltpu.VMEM((CHUNKS, 4, 16, 3 * ff), F32),
            pltpu.VMEM(slot, BF16),
            pltpu.VMEM(slot, BF16),
            pltpu.VMEM(slot, BF16),
            pltpu.VMEM(slot, BF16),
            pltpu.VMEM(slot, BF16),
            pltpu.VMEM(slot, BF16),
            pltpu.VMEM(slot, BF16),
            pltpu.VMEM(slot, BF16),
            pltpu.VMEM(blocks + (3 * ff,), BF16),
            pltpu.VMEM((CHUNKS, 2, 2, 16, feats), F32),
            pltpu.VMEM((CHUNKS, 2, 16, feats), F32),
            pltpu.VMEM((6, 2, 16, feats), F32),
            pltpu.VMEM((6, 2, 16, feats), F32),
            pltpu.VMEM((16, feats), F32),
            pltpu.VMEM((16, feats), F32),
            pltpu.VMEM((2, 16, feats), BF16),
            pltpu.VMEM((2, 16, feats), BF16),
            dma((5,)),
            dma((CHUNKS, PER_CHUNK)),
            dma((CHUNKS, PER_CHUNK)),
            dma((3,)),
            dma((3,)),
            dma((CHUNKS,)),
            dma((CHUNKS,)),
            dma((8,)),
            dma((8,)),
            dma((CHUNKS,)),
            dma((CHUNKS,)),
            dma((6,)),
            dma((6,)),
            dma((3,)),
            dma((3,)),
            dma((CHUNKS, 5)),
        ],
        compiler_params=pltpu.CompilerParams(
            collective_id=0, has_side_effects=True, vmem_limit_bytes=48 * 2**20
        ),
        name="comm",
    )(inputs, out_grad, gate_weight, up_weight, down_weight)

    def flat(a):
        return a.reshape(-1, a.shape[-1])

    def weight_grad(a, b):
        return lax.dot_general(
            flat(a), flat(b), (((0,), (0,)), ((), ())), preferred_element_type=F32
        ).astype(BF16)

    return (
        input_grad,
        weight_grad(x_all, gate_grad),
        weight_grad(x_all, up_grad),
        weight_grad(hidden, d_all),
    )


def solution(mesh):
    return jax.shard_map(
        body,
        mesh=mesh,
        in_specs=(P("col", "row"), P("col", "row"), P("row", "col"), P("row", "col"), P("col", "row")),
        out_specs=(P("col", "row"), P("row", "col"), P("row", "col"), P("col", "row")),
        check_vma=False,
    )
```

```python
import jax
import jax.numpy as jnp
from jax import lax
from jax.experimental import pallas as pl
from jax.experimental.pallas import tpu as pltpu
from jax.sharding import PartitionSpec as P

MESH = pl.DeviceIdType.MESH
BF16 = jnp.bfloat16
F32 = jnp.float32

CHUNKS = 8
CHUNK_OF = ((0, 0), (1, 0), (3, 0), (1, 1), (3, 1), (2, 0), (2, 1), (0, 1))

BEFORE_A = (
    ("g0",),
    ("g2", "b0", "B0", "g1",),
    (),
    ("P", "C0", "g4", "b1", "B1", "g3", "b2", "B2",),
    (),
    ("C1", "C2", "g5",),
    ("b3", "B3",),
    ("b4", "B4", "D0",),
)
BEFORE_G = (
    ("b5", "B5", "C3", "b6", "B6", "D1", "C4", "f0", "F0", "D2", "b7", "B7", "C5", "D3", "C6", "f1", "F1",),
    ("f2", "F2", "D4", "H0", "C7", "f3", "F3", "D5",),
    (),
    ("f4", "F4", "H1", "D6", "H2",),
    ("f5", "F5", "H3", "D7", "f6",),
    ("F6", "H4", "f7",),
    ("F7", "H5",),
    (),
)
LAST = ("H6", "M", "H7",)

RELAY_LO, RELAY_HI, DIRECT_HI, DIRECT_LO, SUM_LO, SUM_HI, ZSUM = range(7)
OWN_UP_LO, OWN_UP_HI, OWN_DN_HI, OWN_DN_LO, FWD_LO, FWD_HI = range(7, 13)
PER_CHUNK = 13
NT = (((1,), (1,)), ((), ()))
TN = (((0,), (0,)), ((), ()))


def comm_kernel(
    x_hbm, dy_hbm, wg_hbm, wu_hbm, wd_hbm,
    own_ref, other_ref, xo_hbm, do_hbm, h_hbm, gg_hbm, ug_hbm,
    xd, wg, wu, wd, part, s_far, s_near, s_sum, s_z, r_relay, r_near, r_sum, r_z, grads,
    ig_part, ig_sib, ig_ysend, ig_yrecv, ig_msend, ig_mrecv,
    load_sem, send, recv, p1_send, p1_recv, sib_send, sib_recv, y_send, y_recv,
    ig_sib_send, ig_sib_recv, ig_y_send, ig_y_recv, ig_z_send, ig_z_recv, out_sem, here,
):
    ff = wg.shape[1]
    width = 3 * ff
    cut = (width // 256) * 128
    lo, hi = pl.ds(0, cut), pl.ds(cut, width - cut)

    row, col = lax.axis_index("row"), lax.axis_index("col")
    x, zh = row // 2, row % 2
    zl, y, k = col // 8, (col // 2) % 4, col % 2
    zlo = zl % 2

    def dev(x=x, zh=zh, zl=zl, y=y, k=k):
        return (x * 2 + zh, zl * 8 + y * 2 + k)

    xp, xm, xf = (x + 1) % 4, (x + 3) % 4, (x + 2) % 4
    up, down = dev(x=xp), dev(x=xm)
    partner = dev(zh=1 - zh)
    yp, ym, yf = dev(y=(y + 1) % 4), dev(y=(y + 3) % 4), dev(y=(y + 2) % 4)
    mate_z = zl + 1 - 2 * zlo
    mate, other_same, other_diff = dev(zl=mate_z), dev(zl=(zl + 2) % 4), dev(zl=(mate_z + 2) % 4)
    sibling = dev(k=1 - k)
    zu, zd = (zh * 4 + zl + 1) % 8, (zh * 4 + zl + 7) % 8
    zp, zm = dev(zh=zu // 4, zl=zu % 4), dev(zh=zd // 4, zl=zd % 4)

    def remote(src, dst, ssem, rsem, target):
        return pltpu.make_async_remote_copy(
            src_ref=src, dst_ref=dst, send_sem=ssem, recv_sem=rsem, device_id=target, device_id_type=MESH
        )

    loads = [
        pltpu.make_async_copy(x_hbm, xd.at[0, k, zlo, 0], load_sem.at[0]),
        pltpu.make_async_copy(dy_hbm, xd.at[0, k, zlo, 1], load_sem.at[1]),
        pltpu.make_async_copy(wg_hbm, wg, load_sem.at[2]),
        pltpu.make_async_copy(wu_hbm, wu, load_sem.at[3]),
        pltpu.make_async_copy(wd_hbm, wd, load_sem.at[4]),
    ]
    for load in loads:
        load.start()

    barrier = pltpu.get_barrier_semaphore()
    near = (up, down, yp, ym, zp, zm, sibling)
    for other in near:
        pl.semaphore_signal(barrier, inc=1, device_id=other, device_id_type=MESH)
    loads[0].wait()
    loads[1].wait()
    pl.semaphore_wait(barrier, len(near))

    def tell(which, target):
        pl.semaphore_signal(here.at[which], inc=1, device_id=target, device_id_type=MESH)

    def told(which):
        pl.semaphore_wait(here.at[which], 1)

    mine = xd.at[0, k, zlo]
    z_gather = [
        remote(mine, xd.at[0, k, zlo], p1_send.at[0], p1_recv.at[0], mate),
        remote(mine, xd.at[7, k, zlo], p1_send.at[1], p1_recv.at[1], other_same),
        remote(mine, xd.at[7, k, zlo], p1_send.at[2], p1_recv.at[2], other_diff),
    ]

    def to_sibling(c):
        return remote(xd.at[c, k], xd.at[c, k], sib_send.at[c], sib_recv.at[c], sibling)

    y_gather = [
        remote(xd.at[0, k], xd.at[2, k], y_send.at[0], y_recv.at[0], yp),
        remote(xd.at[0, k], xd.at[1, k], y_send.at[1], y_recv.at[1], ym),
        remote(xd.at[7, k], xd.at[4, k], y_send.at[2], y_recv.at[2], yp),
        remote(xd.at[7, k], xd.at[3, k], y_send.at[3], y_recv.at[3], ym),
        remote(xd.at[2, k, 0], xd.at[5, k, 0], y_send.at[4], y_recv.at[4], yp),
        remote(xd.at[1, k, 1], xd.at[5, k, 1], y_send.at[5], y_recv.at[5], ym),
        remote(xd.at[4, k, 0], xd.at[6, k, 0], y_send.at[6], y_recv.at[6], yp),
        remote(xd.at[3, k, 1], xd.at[6, k, 1], y_send.at[7], y_recv.at[7], ym),
    ]

    def gather_step(step):
        if step == 0:
            z_gather[0].wait_recv()
            y_gather[0].start()
            y_gather[1].start()
            to_sibling(0).start()
        elif step == 1:
            z_gather[1].wait_recv()
            z_gather[2].wait_recv()
            y_gather[2].start()
            y_gather[3].start()
            to_sibling(7).start()
        elif step == 2:
            y_gather[0].wait_recv()
            y_gather[1].wait_recv()
            y_gather[4].start()
            y_gather[5].start()
            to_sibling(1).start()
            to_sibling(2).start()
        elif step == 3:
            y_gather[2].wait_recv()
            y_gather[3].wait_recv()
            y_gather[6].start()
            y_gather[7].start()
            to_sibling(3).start()
            to_sibling(4).start()
        elif step == 4:
            y_gather[4].wait_recv()
            y_gather[5].wait_recv()
            to_sibling(5).start()
        elif step == 5:
            y_gather[6].wait_recv()
            y_gather[7].wait_recv()
            to_sibling(6).start()

    def copy(c, which):
        ends = {
            RELAY_LO: (s_far.at[c, :, lo], r_relay.at[c, :, lo], up),
            RELAY_HI: (s_far.at[c, :, hi], r_relay.at[c, :, hi], down),
            DIRECT_HI: (s_near.at[c, :, hi], r_near.at[c, :, hi], up),
            DIRECT_LO: (s_near.at[c, :, lo], r_near.at[c, :, lo], down),
            SUM_LO: (s_sum.at[c, :, lo], r_sum.at[c, :, lo], up),
            SUM_HI: (s_sum.at[c, :, hi], r_sum.at[c, :, hi], down),
            ZSUM: (s_z.at[c], r_z.at[c], partner),
            OWN_UP_LO: (grads.at[c, x, :, lo], grads.at[c, x, :, lo], up),
            OWN_UP_HI: (grads.at[c, x, :, hi], grads.at[c, x, :, hi], up),
            OWN_DN_HI: (grads.at[c, x, :, hi], grads.at[c, x, :, hi], down),
            OWN_DN_LO: (grads.at[c, x, :, lo], grads.at[c, x, :, lo], down),
            FWD_LO: (grads.at[c, xm, :, lo], grads.at[c, xm, :, lo], up),
            FWD_HI: (grads.at[c, xp, :, hi], grads.at[c, xp, :, hi], down),
        }
        src, dst, target = ends[which]
        return remote(src, dst, send.at[c, which], recv.at[c, which], target)

    def stage_a(c):
        to_sibling(c).wait_recv()
        xs = xd[c, :, :, 0].reshape(64, -1)
        ds = xd[c, :, :, 1].reshape(64, -1)
        gate = jnp.dot(xs, wg[...], preferred_element_type=F32)
        part[c, :, :, 0:ff] = gate.reshape(4, 16, ff)
        upper = jnp.dot(xs, wu[...], preferred_element_type=F32)
        part[c, :, :, ff : 2 * ff] = upper.reshape(4, 16, ff)
        hgrad = lax.dot_general(ds, wd[...], NT, preferred_element_type=F32)
        part[c, :, :, 2 * ff :] = hgrad.reshape(4, 16, ff)
        s_far[c] = part[c, xf].astype(BF16)
        copy(c, RELAY_LO).start()
        copy(c, RELAY_HI).start()
        s_near[c, :, hi] = part[c, xp, :, hi].astype(BF16)
        s_near[c, :, lo] = part[c, xm, :, lo].astype(BF16)
        copy(c, DIRECT_HI).start()
        copy(c, DIRECT_LO).start()

    def stage_b_lo(c):
        copy(c, RELAY_LO).wait_recv()
        s_sum[c, :, lo] = (part[c, xp, :, lo] + r_relay[c, :, lo].astype(F32)).astype(BF16)
        copy(c, SUM_LO).start()

    def stage_b_hi(c):
        copy(c, RELAY_HI).wait_recv()
        s_sum[c, :, hi] = (part[c, xm, :, hi] + r_relay[c, :, hi].astype(F32)).astype(BF16)
        copy(c, SUM_HI).start()

    def stage_c(c):
        for which in (DIRECT_HI, DIRECT_LO, SUM_LO, SUM_HI):
            copy(c, which).wait_recv()
        total = part[c, x] + r_near[c].astype(F32) + r_sum[c].astype(F32)
        part[c, x] = total
        s_z[c] = total.astype(BF16)
        copy(c, ZSUM).start()

    def stage_d(c):
        copy(c, ZSUM).wait_recv()
        gate = part[c, x, :, 0:ff] + r_z[c, :, 0:ff].astype(F32)
        upper = part[c, x, :, ff : 2 * ff] + r_z[c, :, ff : 2 * ff].astype(F32)
        hgrad = part[c, x, :, 2 * ff :] + r_z[c, :, 2 * ff :].astype(F32)
        sigm = 1.0 / (1.0 + jnp.exp(-gate))
        act = gate * sigm
        grads[c, x, :, 0:ff] = (act * upper).astype(BF16)
        grads[c, x, :, ff : 2 * ff] = (hgrad * upper * sigm * (1.0 + gate * (1.0 - sigm))).astype(BF16)
        grads[c, x, :, 2 * ff :] = (hgrad * act).astype(BF16)
        for which in (OWN_UP_LO, OWN_DN_HI, OWN_UP_HI, OWN_DN_LO):
            copy(c, which).start()

    def stage_f_lo(c):
        copy(c, OWN_UP_LO).wait_recv()
        copy(c, FWD_LO).start()

    def stage_f_hi(c):
        copy(c, OWN_DN_HI).wait_recv()
        copy(c, FWD_HI).start()

    def outs(c):
        return [
            pltpu.make_async_copy(grads.at[c, :, :, pl.ds(0, ff)], h_hbm.at[c], out_sem.at[c, 0]),
            pltpu.make_async_copy(grads.at[c, :, :, pl.ds(ff, ff)], gg_hbm.at[c], out_sem.at[c, 1]),
            pltpu.make_async_copy(grads.at[c, :, :, pl.ds(2 * ff, ff)], ug_hbm.at[c], out_sem.at[c, 2]),
            pltpu.make_async_copy(xd.at[c, :, :, 0], xo_hbm.at[c], out_sem.at[c, 3]),
            pltpu.make_async_copy(xd.at[c, :, :, 1], do_hbm.at[c], out_sem.at[c, 4]),
        ]

    def ig_to_sibling(c):
        return remote(ig_part.at[c, 1 - k], ig_sib.at[c], ig_sib_send.at[c], ig_sib_recv.at[c], sibling)

    def stage_g(c):
        for which in (OWN_UP_HI, OWN_DN_LO, FWD_LO, FWD_HI):
            copy(c, which).wait_recv()
        for out in outs(c):
            out.start()
        gg = grads[c, :, :, ff : 2 * ff].reshape(64, ff)
        ug = grads[c, :, :, 2 * ff :].reshape(64, ff)
        total = lax.dot_general(gg, wg[...], NT, preferred_element_type=F32)
        total = total + lax.dot_general(ug, wu[...], NT, preferred_element_type=F32)
        ig_part[c] = total.reshape(2, 2, 16, -1)
        ig_to_sibling(c).start()

    def ig_to_y(c):
        dy, other = CHUNK_OF[c]
        slot = (dy - 1) * 2 + other
        target = {1: yp, 2: yf, 3: ym}[dy]
        return remote(ig_ysend.at[slot], ig_yrecv.at[slot], ig_y_send.at[slot], ig_y_recv.at[slot], target)

    def stage_h(c):
        ig_to_sibling(c).wait_recv()
        total = ig_part[c, k] + ig_sib[c]
        dy, other = CHUNK_OF[c]
        if dy == 0:
            ig_part[c, k] = total
        else:
            ig_ysend[(dy - 1) * 2 + other] = total
            if c == 5:
                told(5)
            ig_to_y(c).start()

    def own(other, block):
        total = ig_part[7 * other, k, block]
        for dy in range(3):
            total = total + ig_yrecv[dy * 2 + other, block]
        return total

    to_mate = remote(ig_msend, ig_mrecv, ig_z_send, ig_z_recv, mate)

    def send_to_mate():
        for i in (1, 2, 5):
            ig_to_y(i).wait_recv()
        ig_msend[...] = own(0, 1 - zlo)
        to_mate.start()

    z_gather[0].start()
    tell(0, zm)
    tell(1, zp)
    tell(5, ym)
    told(0)
    told(1)
    tell(2, zm)
    tell(3, zp)
    told(2)
    told(3)
    tell(4, zm)
    z_gather[1].start()
    z_gather[2].start()
    for load in loads[2:]:
        load.wait()

    steps = {
        "g": gather_step, "b": stage_b_lo, "B": stage_b_hi, "C": stage_c, "D": stage_d,
        "f": stage_f_lo, "F": stage_f_hi, "H": stage_h,
    }

    def run(names):
        for name in names:
            if name == "M":
                send_to_mate()
            elif name == "P":
                told(4)
            else:
                steps[name[0]](int(name[1]))

    @pl.loop(0, CHUNKS)
    def _(s):
        for i in range(CHUNKS):
            pl.when(s == i)(lambda i=i: run(BEFORE_A[i]))
        stage_a(s)

    @pl.loop(0, CHUNKS)
    def _(s):
        for i in range(CHUNKS):
            pl.when(s == i)(lambda i=i: run(BEFORE_G[i]))
        stage_g(s)

    run(LAST)
    for i in (3, 4, 6):
        ig_to_y(i).wait_recv()
    other_ref[0] = own(1, zlo)
    other_ref[1] = own(1, 1 - zlo)
    to_mate.wait_recv()
    own_ref[...] = own(0, zlo) + ig_mrecv[...]

    for z_copy in z_gather + y_gather + [to_mate]:
        z_copy.wait_send()
    for i in range(1, 7):
        ig_to_y(i).wait_send()

    @pl.loop(0, CHUNKS)
    def _(c):
        for which in range(PER_CHUNK):
            copy(c, which).wait_send()
        to_sibling(c).wait_send()
        ig_to_sibling(c).wait_send()
        for out in outs(c):
            out.wait()


def weight_grad_kernel(
    xv, dv, hv, gv, uv, gate_hbm, up_hbm, down_hbm, gate_up, down, out_sem,
):
    stores = []

    def product(which, lhs, rhs, buffer, target):
        rows = lhs.shape[1]
        for i in range(0, rows, 256):
            part = pl.ds(i, min(256, rows - i))
            buffer[part] = lax.dot_general(lhs[:, part], rhs[...], TN, preferred_element_type=F32).astype(BF16)
            store = pltpu.make_async_copy(buffer.at[part], target.at[part], out_sem.at[which, i // 256])
            store.start()
            stores.append(store)

    product(0, xv, gv, gate_up.at[0], gate_hbm)
    product(1, xv, uv, gate_up.at[1], up_hbm)
    product(2, hv, dv, down, down_hbm)
    for store in stores:
        store.wait()


def body(inputs, out_grad, gate_weight, up_weight, down_weight):
    feats, ff = gate_weight.shape
    blocks = (CHUNKS, 4, 16)
    anywhere = pl.BlockSpec(memory_space=pltpu.HBM)
    slot = (CHUNKS, 16, 3 * ff)
    dma = pltpu.SemaphoreType.DMA
    own, other, x_all, d_all, hidden, gate_grad, up_grad = pl.pallas_call(
        comm_kernel,
        out_shape=[
            jax.ShapeDtypeStruct((16, feats), F32),
            jax.ShapeDtypeStruct((2, 16, feats), F32),
            jax.ShapeDtypeStruct((CHUNKS, 2, 2, 16, feats), BF16),
            jax.ShapeDtypeStruct((CHUNKS, 2, 2, 16, feats), BF16),
            jax.ShapeDtypeStruct(blocks + (ff,), BF16),
            jax.ShapeDtypeStruct(blocks + (ff,), BF16),
            jax.ShapeDtypeStruct(blocks + (ff,), BF16),
        ],
        in_specs=[anywhere] * 5,
        out_specs=[pl.BlockSpec(memory_space=pltpu.VMEM)] * 2 + [anywhere] * 5,
        scratch_shapes=[
            pltpu.VMEM((CHUNKS, 2, 2, 2, 16, feats), BF16),
            pltpu.VMEM((feats, ff), BF16),
            pltpu.VMEM((feats, ff), BF16),
            pltpu.VMEM((ff, feats), BF16),
            pltpu.VMEM((CHUNKS, 4, 16, 3 * ff), F32),
            pltpu.VMEM(slot, BF16),
            pltpu.VMEM(slot, BF16),
            pltpu.VMEM(slot, BF16),
            pltpu.VMEM(slot, BF16),
            pltpu.VMEM(slot, BF16),
            pltpu.VMEM(slot, BF16),
            pltpu.VMEM(slot, BF16),
            pltpu.VMEM(slot, BF16),
            pltpu.VMEM(blocks + (3 * ff,), BF16),
            pltpu.VMEM((CHUNKS, 2, 2, 16, feats), F32),
            pltpu.VMEM((CHUNKS, 2, 16, feats), F32),
            pltpu.VMEM((6, 2, 16, feats), F32),
            pltpu.VMEM((6, 2, 16, feats), F32),
            pltpu.VMEM((16, feats), F32),
            pltpu.VMEM((16, feats), F32),
            dma((5,)),
            dma((CHUNKS, PER_CHUNK)),
            dma((CHUNKS, PER_CHUNK)),
            dma((3,)),
            dma((3,)),
            dma((CHUNKS,)),
            dma((CHUNKS,)),
            dma((8,)),
            dma((8,)),
            dma((CHUNKS,)),
            dma((CHUNKS,)),
            dma((6,)),
            dma((6,)),
            dma(()),
            dma(()),
            dma((CHUNKS, 5)),
            pltpu.SemaphoreType.REGULAR((6,)),
        ],
        compiler_params=pltpu.CompilerParams(
            collective_id=0, has_side_effects=True, vmem_limit_bytes=48 * 2**20
        ),
        name="comm",
    )(*(pltpu.with_memory_space_constraint(a, pltpu.HBM) for a in (inputs, out_grad)), gate_weight, up_weight, down_weight)

    def far(i, col):
        z_lo = col // 8
        target = (z_lo + 2) % 4 if i == 0 else (z_lo + 3 - 2 * (z_lo % 2)) % 4
        return (col, target * 8 + col % 8)

    from_far = [lax.ppermute(other[i], "col", [far(i, col) for col in range(32)]) for i in range(2)]

    def flat(a):
        return a.reshape(-1, a.shape[-1])

    tokens = flat(x_all).shape[0]
    gate_weight_grad, up_weight_grad, down_weight_grad = pl.pallas_call(
        weight_grad_kernel,
        out_shape=[
            jax.ShapeDtypeStruct((feats, ff), BF16),
            jax.ShapeDtypeStruct((feats, ff), BF16),
            jax.ShapeDtypeStruct((ff, feats), BF16),
        ],
        in_specs=[pl.BlockSpec(memory_space=pltpu.VMEM)] * 5,
        out_specs=[anywhere] * 3,
        scratch_shapes=[
            pltpu.VMEM((2, feats, ff), BF16),
            pltpu.VMEM((ff, feats), BF16),
            dma((3, 4)),
        ],
        compiler_params=pltpu.CompilerParams(vmem_limit_bytes=32 * 2**20),
        cost_estimate=pl.CostEstimate(
            flops=6 * tokens * feats * ff,
            bytes_accessed=6 * feats * ff + 2 * tokens * (2 * feats + 3 * ff),
            transcendentals=0,
        ),
        name="weight_grads",
    )(flat(x_all), flat(d_all), flat(hidden), flat(gate_grad), flat(up_grad))
    input_grad = (own + from_far[0] + from_far[1]).astype(BF16)
    return input_grad, gate_weight_grad, up_weight_grad, down_weight_grad


def solution(mesh):
    return jax.shard_map(
        body,
        mesh=mesh,
        in_specs=(P("col", "row"), P("col", "row"), P("row", "col"), P("row", "col"), P("col", "row")),
        out_specs=(P("col", "row"), P("row", "col"), P("row", "col"), P("col", "row")),
        check_vma=False,
    )
```

```python
import jax
import jax.numpy as jnp
from jax import lax
from jax.experimental import pallas as pl
from jax.experimental.pallas import tpu as pltpu
from jax.sharding import PartitionSpec as P

MESH = pl.DeviceIdType.MESH
BF16 = jnp.bfloat16
F32 = jnp.float32

CHUNKS = 8
CHUNK_OF = ((0, 0), (1, 0), (3, 0), (1, 1), (3, 1), (2, 0), (2, 1), (0, 1))

BEFORE_A = (
    ("g0",),
    ("g2", "b0", "B0", "g1",),
    (),
    ("P", "C0", "g4", "b1", "B1", "g3", "b2", "B2",),
    (),
    ("C1", "C2", "g5",),
    ("b3", "B3",),
    ("b4", "B4", "D0",),
)
BEFORE_G = (
    ("b5", "B5", "C3", "b6", "B6", "D1", "C4", "f0", "F0", "D2", "b7", "B7", "C5", "D3", "C6", "f1", "F1",),
    ("f2", "F2", "D4", "H0", "C7", "f3", "F3", "D5",),
    (),
    ("f4", "F4", "H1", "D6", "H2",),
    ("f5", "F5", "H3", "D7", "f6",),
    ("F6", "H4", "f7",),
    ("F7", "H5",),
    ("H6",),
)
LAST = ("M", "H7",)

RELAY_LO, RELAY_HI, DIRECT_HI, DIRECT_LO, SUM_LO, SUM_HI, ZSUM = range(7)
OWN_UP_LO, OWN_UP_HI, OWN_DN_HI, OWN_DN_LO, FWD_LO, FWD_HI = range(7, 13)
PER_CHUNK = 13
NT = (((1,), (1,)), ((), ()))
TN = (((0,), (0,)), ((), ()))


def comm_kernel(
    x_hbm, dy_hbm, wg_hbm, wu_hbm, wd_hbm,
    own_ref, other_ref, xo_hbm, do_hbm, h_hbm, gg_hbm, ug_hbm,
    xd, wg, wu, wd, part, s_far, s_near, s_sum, s_z, r_relay, r_near, r_sum, r_z, grads,
    ig_part, ig_sib, ig_ysend, ig_yrecv, ig_msend, ig_mrecv,
    load_sem, send, recv, p1_send, p1_recv, sib_send, sib_recv, y_send, y_recv,
    ig_sib_send, ig_sib_recv, ig_y_send, ig_y_recv, ig_z_send, ig_z_recv, out_sem, here,
):
    ff = wg.shape[1]
    width = 3 * ff
    cut = (width // 256) * 128
    lo, hi = pl.ds(0, cut), pl.ds(cut, width - cut)

    row, col = lax.axis_index("row"), lax.axis_index("col")
    x, zh = row // 2, row % 2
    zl, y, k = col // 8, (col // 2) % 4, col % 2
    zlo = zl % 2

    def dev(x=x, zh=zh, zl=zl, y=y, k=k):
        return (x * 2 + zh, zl * 8 + y * 2 + k)

    xp, xm, xf = (x + 1) % 4, (x + 3) % 4, (x + 2) % 4
    up, down = dev(x=xp), dev(x=xm)
    partner = dev(zh=1 - zh)
    yp, ym, yf = dev(y=(y + 1) % 4), dev(y=(y + 3) % 4), dev(y=(y + 2) % 4)
    mate_z = zl + 1 - 2 * zlo
    mate, other_same, other_diff = dev(zl=mate_z), dev(zl=(zl + 2) % 4), dev(zl=(mate_z + 2) % 4)
    sibling = dev(k=1 - k)
    zu, zd = (zh * 4 + zl + 1) % 8, (zh * 4 + zl + 7) % 8
    zp, zm = dev(zh=zu // 4, zl=zu % 4), dev(zh=zd // 4, zl=zd % 4)

    def remote(src, dst, ssem, rsem, target):
        return pltpu.make_async_remote_copy(
            src_ref=src, dst_ref=dst, send_sem=ssem, recv_sem=rsem, device_id=target, device_id_type=MESH
        )

    loads = [
        pltpu.make_async_copy(x_hbm, xd.at[0, k, zlo, 0], load_sem.at[0]),
        pltpu.make_async_copy(dy_hbm, xd.at[0, k, zlo, 1], load_sem.at[1]),
        pltpu.make_async_copy(wg_hbm, wg, load_sem.at[2]),
        pltpu.make_async_copy(wu_hbm, wu, load_sem.at[3]),
        pltpu.make_async_copy(wd_hbm, wd, load_sem.at[4]),
    ]
    for load in loads:
        load.start()

    barrier = pltpu.get_barrier_semaphore()
    near = (up, down, yp, ym, zp, zm, sibling)
    for other in near:
        pl.semaphore_signal(barrier, inc=1, device_id=other, device_id_type=MESH)
    loads[0].wait()
    loads[1].wait()
    pl.semaphore_wait(barrier, len(near))

    def tell(which, target):
        pl.semaphore_signal(here.at[which], inc=1, device_id=target, device_id_type=MESH)

    def told(which):
        pl.semaphore_wait(here.at[which], 1)

    mine = xd.at[0, k, zlo]
    z_gather = [
        remote(mine, xd.at[0, k, zlo], p1_send.at[0], p1_recv.at[0], mate),
        remote(mine, xd.at[7, k, zlo], p1_send.at[1], p1_recv.at[1], other_same),
        remote(mine, xd.at[7, k, zlo], p1_send.at[2], p1_recv.at[2], other_diff),
    ]

    def to_sibling(c):
        return remote(xd.at[c, k], xd.at[c, k], sib_send.at[c], sib_recv.at[c], sibling)

    y_gather = [
        remote(xd.at[0, k], xd.at[2, k], y_send.at[0], y_recv.at[0], yp),
        remote(xd.at[0, k], xd.at[1, k], y_send.at[1], y_recv.at[1], ym),
        remote(xd.at[7, k], xd.at[4, k], y_send.at[2], y_recv.at[2], yp),
        remote(xd.at[7, k], xd.at[3, k], y_send.at[3], y_recv.at[3], ym),
        remote(xd.at[2, k, 0], xd.at[5, k, 0], y_send.at[4], y_recv.at[4], yp),
        remote(xd.at[1, k, 1], xd.at[5, k, 1], y_send.at[5], y_recv.at[5], ym),
        remote(xd.at[4, k, 0], xd.at[6, k, 0], y_send.at[6], y_recv.at[6], yp),
        remote(xd.at[3, k, 1], xd.at[6, k, 1], y_send.at[7], y_recv.at[7], ym),
    ]

    def gather_step(step):
        if step == 0:
            z_gather[0].wait_recv()
            y_gather[0].start()
            y_gather[1].start()
            to_sibling(0).start()
        elif step == 1:
            z_gather[1].wait_recv()
            z_gather[2].wait_recv()
            y_gather[2].start()
            y_gather[3].start()
            to_sibling(7).start()
        elif step == 2:
            y_gather[0].wait_recv()
            y_gather[1].wait_recv()
            y_gather[4].start()
            y_gather[5].start()
            to_sibling(1).start()
            to_sibling(2).start()
        elif step == 3:
            y_gather[2].wait_recv()
            y_gather[3].wait_recv()
            y_gather[6].start()
            y_gather[7].start()
            to_sibling(3).start()
            to_sibling(4).start()
        elif step == 4:
            y_gather[4].wait_recv()
            y_gather[5].wait_recv()
            to_sibling(5).start()
        elif step == 5:
            y_gather[6].wait_recv()
            y_gather[7].wait_recv()
            to_sibling(6).start()

    def copy(c, which):
        ends = {
            RELAY_LO: (s_far.at[c, :, lo], r_relay.at[c, :, lo], up),
            RELAY_HI: (s_far.at[c, :, hi], r_relay.at[c, :, hi], down),
            DIRECT_HI: (s_near.at[c, :, hi], r_near.at[c, :, hi], up),
            DIRECT_LO: (s_near.at[c, :, lo], r_near.at[c, :, lo], down),
            SUM_LO: (s_sum.at[c, :, lo], r_sum.at[c, :, lo], up),
            SUM_HI: (s_sum.at[c, :, hi], r_sum.at[c, :, hi], down),
            ZSUM: (s_z.at[c], r_z.at[c], partner),
            OWN_UP_LO: (grads.at[c, x, :, lo], grads.at[c, x, :, lo], up),
            OWN_UP_HI: (grads.at[c, x, :, hi], grads.at[c, x, :, hi], up),
            OWN_DN_HI: (grads.at[c, x, :, hi], grads.at[c, x, :, hi], down),
            OWN_DN_LO: (grads.at[c, x, :, lo], grads.at[c, x, :, lo], down),
            FWD_LO: (grads.at[c, xm, :, lo], grads.at[c, xm, :, lo], up),
            FWD_HI: (grads.at[c, xp, :, hi], grads.at[c, xp, :, hi], down),
        }
        src, dst, target = ends[which]
        return remote(src, dst, send.at[c, which], recv.at[c, which], target)

    def stage_a(c):
        to_sibling(c).wait_recv()
        xs = xd[c, :, :, 0].reshape(64, -1)
        ds = xd[c, :, :, 1].reshape(64, -1)
        gate = jnp.dot(xs, wg[...], preferred_element_type=F32)
        part[c, :, :, 0:ff] = gate.reshape(4, 16, ff)
        upper = jnp.dot(xs, wu[...], preferred_element_type=F32)
        part[c, :, :, ff : 2 * ff] = upper.reshape(4, 16, ff)
        hgrad = lax.dot_general(ds, wd[...], NT, preferred_element_type=F32)
        part[c, :, :, 2 * ff :] = hgrad.reshape(4, 16, ff)
        s_far[c] = part[c, xf].astype(BF16)
        copy(c, RELAY_LO).start()
        copy(c, RELAY_HI).start()
        s_near[c, :, hi] = part[c, xp, :, hi].astype(BF16)
        s_near[c, :, lo] = part[c, xm, :, lo].astype(BF16)
        copy(c, DIRECT_HI).start()
        copy(c, DIRECT_LO).start()

    def stage_b_lo(c):
        copy(c, RELAY_LO).wait_recv()
        s_sum[c, :, lo] = (part[c, xp, :, lo] + r_relay[c, :, lo].astype(F32)).astype(BF16)
        copy(c, SUM_LO).start()

    def stage_b_hi(c):
        copy(c, RELAY_HI).wait_recv()
        s_sum[c, :, hi] = (part[c, xm, :, hi] + r_relay[c, :, hi].astype(F32)).astype(BF16)
        copy(c, SUM_HI).start()

    def stage_c(c):
        for which in (DIRECT_HI, DIRECT_LO, SUM_LO, SUM_HI):
            copy(c, which).wait_recv()
        total = part[c, x] + r_near[c].astype(F32) + r_sum[c].astype(F32)
        part[c, x] = total
        s_z[c] = total.astype(BF16)
        copy(c, ZSUM).start()

    def stage_d(c):
        copy(c, ZSUM).wait_recv()
        gate = part[c, x, :, 0:ff] + r_z[c, :, 0:ff].astype(F32)
        upper = part[c, x, :, ff : 2 * ff] + r_z[c, :, ff : 2 * ff].astype(F32)
        hgrad = part[c, x, :, 2 * ff :] + r_z[c, :, 2 * ff :].astype(F32)
        sigm = 1.0 / (1.0 + jnp.exp(-gate))
        act = gate * sigm
        grads[c, x, :, 0:ff] = (act * upper).astype(BF16)
        grads[c, x, :, ff : 2 * ff] = (hgrad * upper * sigm * (1.0 + gate * (1.0 - sigm))).astype(BF16)
        grads[c, x, :, 2 * ff :] = (hgrad * act).astype(BF16)
        for which in (OWN_UP_LO, OWN_DN_HI, OWN_UP_HI, OWN_DN_LO):
            copy(c, which).start()

    def stage_f_lo(c):
        copy(c, OWN_UP_LO).wait_recv()
        copy(c, FWD_LO).start()

    def stage_f_hi(c):
        copy(c, OWN_DN_HI).wait_recv()
        copy(c, FWD_HI).start()

    def outs(c):
        return [
            pltpu.make_async_copy(grads.at[c, :, :, pl.ds(0, ff)], h_hbm.at[c], out_sem.at[c, 0]),
            pltpu.make_async_copy(grads.at[c, :, :, pl.ds(ff, ff)], gg_hbm.at[c], out_sem.at[c, 1]),
            pltpu.make_async_copy(grads.at[c, :, :, pl.ds(2 * ff, ff)], ug_hbm.at[c], out_sem.at[c, 2]),
            pltpu.make_async_copy(xd.at[c, :, :, 0], xo_hbm.at[c], out_sem.at[c, 3]),
            pltpu.make_async_copy(xd.at[c, :, :, 1], do_hbm.at[c], out_sem.at[c, 4]),
        ]

    def ig_to_sibling(c):
        return remote(ig_part.at[c, 1 - k], ig_sib.at[c], ig_sib_send.at[c], ig_sib_recv.at[c], sibling)

    def stage_g(c):
        for which in (OWN_UP_HI, OWN_DN_LO, FWD_LO, FWD_HI):
            copy(c, which).wait_recv()
        for out in outs(c):
            out.start()
        gg = grads[c, :, :, ff : 2 * ff].reshape(64, ff)
        ug = grads[c, :, :, 2 * ff :].reshape(64, ff)
        total = lax.dot_general(gg, wg[...], NT, preferred_element_type=F32)
        total = total + lax.dot_general(ug, wu[...], NT, preferred_element_type=F32)
        ig_part[c] = total.reshape(2, 2, 16, -1)
        ig_to_sibling(c).start()

    def ig_to_y(c):
        dy, other = CHUNK_OF[c]
        slot = (dy - 1) * 2 + other
        target = {1: yp, 2: yf, 3: ym}[dy]
        return remote(ig_ysend.at[slot], ig_yrecv.at[slot], ig_y_send.at[slot], ig_y_recv.at[slot], target)

    def stage_h(c):
        ig_to_sibling(c).wait_recv()
        total = ig_part[c, k] + ig_sib[c]
        dy, other = CHUNK_OF[c]
        if dy == 0:
            ig_part[c, k] = total
        else:
            ig_ysend[(dy - 1) * 2 + other] = total
            if c == 5:
                told(5)
            ig_to_y(c).start()

    def own(other, block):
        total = ig_part[7 * other, k, block]
        for dy in range(3):
            total = total + ig_yrecv[dy * 2 + other, block]
        return total

    to_mate = remote(ig_msend, ig_mrecv, ig_z_send, ig_z_recv, mate)

    def send_to_mate():
        for i in (1, 2, 5):
            ig_to_y(i).wait_recv()
        ig_msend[...] = own(0, 1 - zlo)
        to_mate.start()

    z_gather[0].start()
    tell(0, zm)
    tell(1, zp)
    tell(5, ym)
    told(0)
    told(1)
    tell(2, zm)
    tell(3, zp)
    told(2)
    told(3)
    tell(4, zm)
    z_gather[1].start()
    z_gather[2].start()
    for load in loads[2:]:
        load.wait()

    def drain(c):
        for which in range(PER_CHUNK):
            copy(c, which).wait_send()
        to_sibling(c).wait_send()
        ig_to_sibling(c).wait_send()
        for out in outs(c):
            out.wait()

    steps = {
        "g": gather_step, "b": stage_b_lo, "B": stage_b_hi, "C": stage_c, "D": stage_d,
        "f": stage_f_lo, "F": stage_f_hi, "H": stage_h,
    }

    def run(names):
        for name in names:
            if name == "M":
                send_to_mate()
            elif name == "P":
                told(4)
            else:
                steps[name[0]](int(name[1]))

    @pl.loop(0, CHUNKS)
    def _(s):
        for i in range(CHUNKS):
            pl.when(s == i)(lambda i=i: run(BEFORE_A[i]))
        stage_a(s)

    @pl.loop(0, CHUNKS)
    def _(s):
        for i in range(CHUNKS):
            pl.when(s == i)(lambda i=i: run(BEFORE_G[i]))

        @pl.when(s >= 2)
        def _():
            drain(s - 2)

        stage_g(s)

    run(LAST)
    for i in (3, 4, 6):
        ig_to_y(i).wait_recv()
    other_ref[0] = own(1, zlo)
    other_ref[1] = own(1, 1 - zlo)
    to_mate.wait_recv()
    own_ref[...] = own(0, zlo) + ig_mrecv[...]

    for z_copy in z_gather + y_gather + [to_mate]:
        z_copy.wait_send()
    for i in range(1, 7):
        ig_to_y(i).wait_send()

    for c in (CHUNKS - 2, CHUNKS - 1):
        drain(c)


def weight_grad_kernel(
    xv, dv, hv, gv, uv, gate_hbm, up_hbm, down_hbm, gate_up, down, out_sem,
):
    stores = []

    def product(which, lhs, rhs, buffer, target):
        rows = lhs.shape[1]
        for i in range(0, rows, 256):
            part = pl.ds(i, min(256, rows - i))
            buffer[part] = lax.dot_general(lhs[:, part], rhs[...], TN, preferred_element_type=F32).astype(BF16)
            store = pltpu.make_async_copy(buffer.at[part], target.at[part], out_sem.at[which, i // 256])
            store.start()
            stores.append(store)

    product(0, xv, gv, gate_up.at[0], gate_hbm)
    product(1, xv, uv, gate_up.at[1], up_hbm)
    product(2, hv, dv, down, down_hbm)
    for store in stores:
        store.wait()


def body(inputs, out_grad, gate_weight, up_weight, down_weight):
    feats, ff = gate_weight.shape
    blocks = (CHUNKS, 4, 16)
    anywhere = pl.BlockSpec(memory_space=pltpu.HBM)
    slot = (CHUNKS, 16, 3 * ff)
    dma = pltpu.SemaphoreType.DMA
    own, other, x_all, d_all, hidden, gate_grad, up_grad = pl.pallas_call(
        comm_kernel,
        out_shape=[
            jax.ShapeDtypeStruct((16, feats), F32),
            jax.ShapeDtypeStruct((2, 16, feats), F32),
            jax.ShapeDtypeStruct((CHUNKS, 2, 2, 16, feats), BF16),
            jax.ShapeDtypeStruct((CHUNKS, 2, 2, 16, feats), BF16),
            jax.ShapeDtypeStruct(blocks + (ff,), BF16),
            jax.ShapeDtypeStruct(blocks + (ff,), BF16),
            jax.ShapeDtypeStruct(blocks + (ff,), BF16),
        ],
        in_specs=[anywhere] * 5,
        out_specs=[pl.BlockSpec(memory_space=pltpu.VMEM)] * 2 + [anywhere] * 5,
        scratch_shapes=[
            pltpu.VMEM((CHUNKS, 2, 2, 2, 16, feats), BF16),
            pltpu.VMEM((feats, ff), BF16),
            pltpu.VMEM((feats, ff), BF16),
            pltpu.VMEM((ff, feats), BF16),
            pltpu.VMEM((CHUNKS, 4, 16, 3 * ff), F32),
            pltpu.VMEM(slot, BF16),
            pltpu.VMEM(slot, BF16),
            pltpu.VMEM(slot, BF16),
            pltpu.VMEM(slot, BF16),
            pltpu.VMEM(slot, BF16),
            pltpu.VMEM(slot, BF16),
            pltpu.VMEM(slot, BF16),
            pltpu.VMEM(slot, BF16),
            pltpu.VMEM(blocks + (3 * ff,), BF16),
            pltpu.VMEM((CHUNKS, 2, 2, 16, feats), F32),
            pltpu.VMEM((CHUNKS, 2, 16, feats), F32),
            pltpu.VMEM((6, 2, 16, feats), F32),
            pltpu.VMEM((6, 2, 16, feats), F32),
            pltpu.VMEM((16, feats), F32),
            pltpu.VMEM((16, feats), F32),
            dma((5,)),
            dma((CHUNKS, PER_CHUNK)),
            dma((CHUNKS, PER_CHUNK)),
            dma((3,)),
            dma((3,)),
            dma((CHUNKS,)),
            dma((CHUNKS,)),
            dma((8,)),
            dma((8,)),
            dma((CHUNKS,)),
            dma((CHUNKS,)),
            dma((6,)),
            dma((6,)),
            dma(()),
            dma(()),
            dma((CHUNKS, 5)),
            pltpu.SemaphoreType.REGULAR((6,)),
        ],
        compiler_params=pltpu.CompilerParams(
            collective_id=0, has_side_effects=True, vmem_limit_bytes=48 * 2**20
        ),
        name="comm",
    )(*(pltpu.with_memory_space_constraint(a, pltpu.HBM) for a in (inputs, out_grad)), gate_weight, up_weight, down_weight)

    def far(i, col):
        z_lo = col // 8
        target = (z_lo + 2) % 4 if i == 0 else (z_lo + 3 - 2 * (z_lo % 2)) % 4
        return (col, target * 8 + col % 8)

    from_far = [lax.ppermute(other[i], "col", [far(i, col) for col in range(32)]) for i in range(2)]

    def flat(a):
        return a.reshape(-1, a.shape[-1])

    tokens = flat(x_all).shape[0]
    gate_weight_grad, up_weight_grad, down_weight_grad = pl.pallas_call(
        weight_grad_kernel,
        out_shape=[
            jax.ShapeDtypeStruct((feats, ff), BF16),
            jax.ShapeDtypeStruct((feats, ff), BF16),
            jax.ShapeDtypeStruct((ff, feats), BF16),
        ],
        in_specs=[pl.BlockSpec(memory_space=pltpu.VMEM)] * 5,
        out_specs=[anywhere] * 3,
        scratch_shapes=[
            pltpu.VMEM((2, feats, ff), BF16),
            pltpu.VMEM((ff, feats), BF16),
            dma((3, 4)),
        ],
        compiler_params=pltpu.CompilerParams(vmem_limit_bytes=32 * 2**20),
        cost_estimate=pl.CostEstimate(
            flops=6 * tokens * feats * ff,
            bytes_accessed=6 * feats * ff + 2 * tokens * (2 * feats + 3 * ff),
            transcendentals=0,
        ),
        name="weight_grads",
    )(flat(x_all), flat(d_all), flat(hidden), flat(gate_grad), flat(up_grad))
    input_grad = (own + from_far[0] + from_far[1]).astype(BF16)
    return input_grad, gate_weight_grad, up_weight_grad, down_weight_grad


def solution(mesh):
    return jax.shard_map(
        body,
        mesh=mesh,
        in_specs=(P("col", "row"), P("col", "row"), P("row", "col"), P("row", "col"), P("col", "row")),
        out_specs=(P("col", "row"), P("row", "col"), P("row", "col"), P("col", "row")),
        check_vma=False,
    )
```

```python
import jax
import jax.numpy as jnp
from jax import lax
from jax.experimental import pallas as pl
from jax.experimental.pallas import tpu as pltpu
from jax.sharding import PartitionSpec as P

MESH = pl.DeviceIdType.MESH
BF16 = jnp.bfloat16
F32 = jnp.float32

CHUNKS = 8
CHUNK_OF = ((0, 0), (1, 0), (3, 0), (1, 1), (3, 1), (2, 0), (2, 1), (0, 1))

BEFORE_A = (
    ("g0",),
    ("g2", "b0", "B0", "g1",),
    (),
    ("P", "C0", "g4", "b1", "B1", "g3", "b2", "B2",),
    (),
    ("C1", "C2", "g5",),
    ("b3", "B3",),
    ("b4", "B4", "D0",),
)
BEFORE_G = (
    ("b5", "B5", "C3", "b6", "B6", "D1", "C4", "f0", "F0", "D2", "b7", "B7", "C5", "D3", "C6", "f1", "F1",),
    ("f2", "F2", "D4", "H0", "C7", "f3", "F3", "D5",),
    (),
    ("f4", "F4", "H1", "D6", "H2",),
    ("f5", "F5", "H3", "D7", "f6",),
    ("F6", "H4", "f7",),
    ("F7", "H5",),
    ("H6",),
)
LAST = ("M", "H7",)

RELAY_LO, RELAY_HI, DIRECT_HI, DIRECT_LO, SUM_LO, SUM_HI, ZSUM = range(7)
OWN_UP_LO, OWN_UP_HI, OWN_DN_HI, OWN_DN_LO, FWD_LO, FWD_HI = range(7, 13)
PER_CHUNK = 13
NT = (((1,), (1,)), ((), ()))
TN = (((0,), (0,)), ((), ()))


def comm_kernel(
    x_hbm, dy_hbm, wg_hbm, wu_hbm, wd_hbm,
    own_ref, other_ref, xo_hbm, do_hbm, h_hbm, gu_hbm,
    xd, wg, wu, wd, part, s_far, s_near, s_sum, s_z, r_relay, r_near, r_sum, r_z, grads,
    ig_part, ig_sib, ig_ysend, ig_yrecv, ig_msend, ig_mrecv,
    load_sem, send, recv, p1_send, p1_recv, sib_send, sib_recv, y_send, y_recv,
    ig_sib_send, ig_sib_recv, ig_y_send, ig_y_recv, ig_z_send, ig_z_recv, out_sem, here,
):
    ff = wg.shape[1]
    width = 3 * ff
    cut = (width // 256) * 128
    lo, hi = pl.ds(0, cut), pl.ds(cut, width - cut)

    row, col = lax.axis_index("row"), lax.axis_index("col")
    x, zh = row // 2, row % 2
    zl, y, k = col // 8, (col // 2) % 4, col % 2
    zlo = zl % 2

    def dev(x=x, zh=zh, zl=zl, y=y, k=k):
        return (x * 2 + zh, zl * 8 + y * 2 + k)

    xp, xm, xf = (x + 1) % 4, (x + 3) % 4, (x + 2) % 4
    up, down = dev(x=xp), dev(x=xm)
    partner = dev(zh=1 - zh)
    yp, ym, yf = dev(y=(y + 1) % 4), dev(y=(y + 3) % 4), dev(y=(y + 2) % 4)
    mate_z = zl + 1 - 2 * zlo
    mate, other_same, other_diff = dev(zl=mate_z), dev(zl=(zl + 2) % 4), dev(zl=(mate_z + 2) % 4)
    sibling = dev(k=1 - k)
    zu, zd = (zh * 4 + zl + 1) % 8, (zh * 4 + zl + 7) % 8
    zp, zm = dev(zh=zu // 4, zl=zu % 4), dev(zh=zd // 4, zl=zd % 4)

    def remote(src, dst, ssem, rsem, target):
        return pltpu.make_async_remote_copy(
            src_ref=src, dst_ref=dst, send_sem=ssem, recv_sem=rsem, device_id=target, device_id_type=MESH
        )

    loads = [
        pltpu.make_async_copy(x_hbm, xd.at[0, k, zlo, 0], load_sem.at[0]),
        pltpu.make_async_copy(dy_hbm, xd.at[0, k, zlo, 1], load_sem.at[1]),
        pltpu.make_async_copy(wg_hbm, wg, load_sem.at[2]),
        pltpu.make_async_copy(wu_hbm, wu, load_sem.at[3]),
        pltpu.make_async_copy(wd_hbm, wd, load_sem.at[4]),
    ]
    for load in loads:
        load.start()

    barrier = pltpu.get_barrier_semaphore()
    near = (up, down, yp, ym, zp, zm, sibling)
    for other in near:
        pl.semaphore_signal(barrier, inc=1, device_id=other, device_id_type=MESH)
    loads[0].wait()
    loads[1].wait()
    pl.semaphore_wait(barrier, len(near))

    def tell(which, target):
        pl.semaphore_signal(here.at[which], inc=1, device_id=target, device_id_type=MESH)

    def told(which):
        pl.semaphore_wait(here.at[which], 1)

    mine = xd.at[0, k, zlo]
    z_gather = [
        remote(mine, xd.at[0, k, zlo], p1_send.at[0], p1_recv.at[0], mate),
        remote(mine, xd.at[7, k, zlo], p1_send.at[1], p1_recv.at[1], other_same),
        remote(mine, xd.at[7, k, zlo], p1_send.at[2], p1_recv.at[2], other_diff),
    ]

    def to_sibling(c):
        return remote(xd.at[c, k], xd.at[c, k], sib_send.at[c], sib_recv.at[c], sibling)

    y_gather = [
        remote(xd.at[0, k], xd.at[2, k], y_send.at[0], y_recv.at[0], yp),
        remote(xd.at[0, k], xd.at[1, k], y_send.at[1], y_recv.at[1], ym),
        remote(xd.at[7, k], xd.at[4, k], y_send.at[2], y_recv.at[2], yp),
        remote(xd.at[7, k], xd.at[3, k], y_send.at[3], y_recv.at[3], ym),
        remote(xd.at[2, k, 0], xd.at[5, k, 0], y_send.at[4], y_recv.at[4], yp),
        remote(xd.at[1, k, 1], xd.at[5, k, 1], y_send.at[5], y_recv.at[5], ym),
        remote(xd.at[4, k, 0], xd.at[6, k, 0], y_send.at[6], y_recv.at[6], yp),
        remote(xd.at[3, k, 1], xd.at[6, k, 1], y_send.at[7], y_recv.at[7], ym),
    ]

    def gather_step(step):
        if step == 0:
            z_gather[0].wait_recv()
            y_gather[0].start()
            y_gather[1].start()
            to_sibling(0).start()
        elif step == 1:
            z_gather[1].wait_recv()
            z_gather[2].wait_recv()
            y_gather[2].start()
            y_gather[3].start()
            to_sibling(7).start()
        elif step == 2:
            y_gather[0].wait_recv()
            y_gather[1].wait_recv()
            y_gather[4].start()
            y_gather[5].start()
            to_sibling(1).start()
            to_sibling(2).start()
        elif step == 3:
            y_gather[2].wait_recv()
            y_gather[3].wait_recv()
            y_gather[6].start()
            y_gather[7].start()
            to_sibling(3).start()
            to_sibling(4).start()
        elif step == 4:
            y_gather[4].wait_recv()
            y_gather[5].wait_recv()
            to_sibling(5).start()
        elif step == 5:
            y_gather[6].wait_recv()
            y_gather[7].wait_recv()
            to_sibling(6).start()

    def copy(c, which):
        ends = {
            RELAY_LO: (s_far.at[c, :, lo], r_relay.at[c, :, lo], up),
            RELAY_HI: (s_far.at[c, :, hi], r_relay.at[c, :, hi], down),
            DIRECT_HI: (s_near.at[c, :, hi], r_near.at[c, :, hi], up),
            DIRECT_LO: (s_near.at[c, :, lo], r_near.at[c, :, lo], down),
            SUM_LO: (s_sum.at[c, :, lo], r_sum.at[c, :, lo], up),
            SUM_HI: (s_sum.at[c, :, hi], r_sum.at[c, :, hi], down),
            ZSUM: (s_z.at[c], r_z.at[c], partner),
            OWN_UP_LO: (grads.at[c, x, :, lo], grads.at[c, x, :, lo], up),
            OWN_UP_HI: (grads.at[c, x, :, hi], grads.at[c, x, :, hi], up),
            OWN_DN_HI: (grads.at[c, x, :, hi], grads.at[c, x, :, hi], down),
            OWN_DN_LO: (grads.at[c, x, :, lo], grads.at[c, x, :, lo], down),
            FWD_LO: (grads.at[c, xm, :, lo], grads.at[c, xm, :, lo], up),
            FWD_HI: (grads.at[c, xp, :, hi], grads.at[c, xp, :, hi], down),
        }
        src, dst, target = ends[which]
        return remote(src, dst, send.at[c, which], recv.at[c, which], target)

    def stage_a(c):
        to_sibling(c).wait_recv()
        xs = xd[c, :, :, 0].reshape(64, -1)
        ds = xd[c, :, :, 1].reshape(64, -1)
        gate = jnp.dot(xs, wg[...], preferred_element_type=F32)
        part[c, :, :, 0:ff] = gate.reshape(4, 16, ff)
        upper = jnp.dot(xs, wu[...], preferred_element_type=F32)
        part[c, :, :, ff : 2 * ff] = upper.reshape(4, 16, ff)
        hgrad = lax.dot_general(ds, wd[...], NT, preferred_element_type=F32)
        part[c, :, :, 2 * ff :] = hgrad.reshape(4, 16, ff)
        s_far[c] = part[c, xf].astype(BF16)
        copy(c, RELAY_LO).start()
        copy(c, RELAY_HI).start()
        s_near[c, :, hi] = part[c, xp, :, hi].astype(BF16)
        s_near[c, :, lo] = part[c, xm, :, lo].astype(BF16)
        copy(c, DIRECT_HI).start()
        copy(c, DIRECT_LO).start()

    def stage_b_lo(c):
        copy(c, RELAY_LO).wait_recv()
        s_sum[c, :, lo] = (part[c, xp, :, lo] + r_relay[c, :, lo].astype(F32)).astype(BF16)
        copy(c, SUM_LO).start()

    def stage_b_hi(c):
        copy(c, RELAY_HI).wait_recv()
        s_sum[c, :, hi] = (part[c, xm, :, hi] + r_relay[c, :, hi].astype(F32)).astype(BF16)
        copy(c, SUM_HI).start()

    def stage_c(c):
        for which in (DIRECT_HI, DIRECT_LO, SUM_LO, SUM_HI):
            copy(c, which).wait_recv()
        total = part[c, x] + r_near[c].astype(F32) + r_sum[c].astype(F32)
        part[c, x] = total
        s_z[c] = total.astype(BF16)
        copy(c, ZSUM).start()

    def stage_d(c):
        copy(c, ZSUM).wait_recv()
        gate = part[c, x, :, 0:ff] + r_z[c, :, 0:ff].astype(F32)
        upper = part[c, x, :, ff : 2 * ff] + r_z[c, :, ff : 2 * ff].astype(F32)
        hgrad = part[c, x, :, 2 * ff :] + r_z[c, :, 2 * ff :].astype(F32)
        sigm = 1.0 / (1.0 + jnp.exp(-gate))
        act = gate * sigm
        grads[c, x, :, 0:ff] = (act * upper).astype(BF16)
        grads[c, x, :, ff : 2 * ff] = (hgrad * upper * sigm * (1.0 + gate * (1.0 - sigm))).astype(BF16)
        grads[c, x, :, 2 * ff :] = (hgrad * act).astype(BF16)
        for which in (OWN_UP_LO, OWN_DN_HI, OWN_UP_HI, OWN_DN_LO):
            copy(c, which).start()

    def stage_f_lo(c):
        copy(c, OWN_UP_LO).wait_recv()
        copy(c, FWD_LO).start()

    def stage_f_hi(c):
        copy(c, OWN_DN_HI).wait_recv()
        copy(c, FWD_HI).start()

    def outs(c):
        return [
            pltpu.make_async_copy(grads.at[c, :, :, pl.ds(0, ff)], h_hbm.at[c], out_sem.at[c, 0]),
            pltpu.make_async_copy(grads.at[c, :, :, pl.ds(ff, 2 * ff)], gu_hbm.at[c], out_sem.at[c, 1]),
            pltpu.make_async_copy(xd.at[c, :, :, 0], xo_hbm.at[c], out_sem.at[c, 2]),
            pltpu.make_async_copy(xd.at[c, :, :, 1], do_hbm.at[c], out_sem.at[c, 3]),
        ]

    def ig_to_sibling(c):
        return remote(ig_part.at[c, 1 - k], ig_sib.at[c], ig_sib_send.at[c], ig_sib_recv.at[c], sibling)

    def stage_g(c):
        for which in (OWN_UP_HI, OWN_DN_LO, FWD_LO, FWD_HI):
            copy(c, which).wait_recv()
        for out in outs(c):
            out.start()
        gg = grads[c, :, :, ff : 2 * ff].reshape(64, ff)
        ug = grads[c, :, :, 2 * ff :].reshape(64, ff)
        total = lax.dot_general(gg, wg[...], NT, preferred_element_type=F32)
        total = total + lax.dot_general(ug, wu[...], NT, preferred_element_type=F32)
        ig_part[c] = total.reshape(2, 2, 16, -1)
        ig_to_sibling(c).start()

    def ig_to_y(c):
        dy, other = CHUNK_OF[c]
        slot = (dy - 1) * 2 + other
        target = {1: yp, 2: yf, 3: ym}[dy]
        return remote(ig_ysend.at[slot], ig_yrecv.at[slot], ig_y_send.at[slot], ig_y_recv.at[slot], target)

    def stage_h(c):
        ig_to_sibling(c).wait_recv()
        total = ig_part[c, k] + ig_sib[c]
        dy, other = CHUNK_OF[c]
        if dy == 0:
            ig_part[c, k] = total
        else:
            ig_ysend[(dy - 1) * 2 + other] = total
            if c == 5:
                told(5)
            ig_to_y(c).start()

    def own(other, block):
        total = ig_part[7 * other, k, block]
        for dy in range(3):
            total = total + ig_yrecv[dy * 2 + other, block]
        return total

    to_mate = remote(ig_msend, ig_mrecv, ig_z_send, ig_z_recv, mate)

    def send_to_mate():
        for i in (1, 2, 5):
            ig_to_y(i).wait_recv()
        ig_msend[...] = own(0, 1 - zlo)
        to_mate.start()

    z_gather[0].start()
    tell(0, zm)
    tell(1, zp)
    tell(5, ym)
    told(0)
    told(1)
    tell(2, zm)
    tell(3, zp)
    told(2)
    told(3)
    tell(4, zm)
    z_gather[1].start()
    z_gather[2].start()
    for load in loads[2:]:
        load.wait()

    def drain(c):
        for which in range(PER_CHUNK):
            copy(c, which).wait_send()
        to_sibling(c).wait_send()
        ig_to_sibling(c).wait_send()
        for out in outs(c):
            out.wait()

    steps = {
        "g": gather_step, "b": stage_b_lo, "B": stage_b_hi, "C": stage_c, "D": stage_d,
        "f": stage_f_lo, "F": stage_f_hi, "H": stage_h,
    }

    def run(names):
        for name in names:
            if name == "M":
                send_to_mate()
            elif name == "P":
                told(4)
            else:
                steps[name[0]](int(name[1]))

    @pl.loop(0, CHUNKS)
    def _(s):
        for i in range(CHUNKS):
            pl.when(s == i)(lambda i=i: run(BEFORE_A[i]))
        stage_a(s)

    @pl.loop(0, CHUNKS)
    def _(s):
        for i in range(CHUNKS):
            pl.when(s == i)(lambda i=i: run(BEFORE_G[i]))

        @pl.when(s >= 2)
        def _():
            drain(s - 2)

        stage_g(s)

    run(LAST)
    for i in (3, 4, 6):
        ig_to_y(i).wait_recv()
    other_ref[0] = own(1, zlo)
    other_ref[1] = own(1, 1 - zlo)
    to_mate.wait_recv()
    own_ref[...] = own(0, zlo) + ig_mrecv[...]

    for z_copy in z_gather + y_gather + [to_mate]:
        z_copy.wait_send()
    for i in range(1, 7):
        ig_to_y(i).wait_send()

    for c in (CHUNKS - 2, CHUNKS - 1):
        drain(c)


def weight_grad_kernel(xv, dv, hv, guv, gate_hbm, up_hbm, down_hbm, gate, up, down, out_sem):
    ff = hv.shape[1]
    stores = []

    def product(lhs, rhs, i, targets):
        part = pl.ds(i, min(256, lhs.shape[1] - i))
        total = lax.dot_general(lhs[:, part], rhs[...], TN, preferred_element_type=F32)
        width = total.shape[1] // len(targets)
        for n, (which, buffer, target) in enumerate(targets):
            buffer[part] = total[:, n * width : (n + 1) * width].astype(BF16)
            store = pltpu.make_async_copy(buffer.at[part], target.at[part], out_sem.at[which, i // 256])
            store.start()
            stores.append(store)

    for i in range(0, xv.shape[1], 256):
        product(xv, guv, i, ((0, gate, gate_hbm), (1, up, up_hbm)))
    for i in range(0, ff, 256):
        product(hv, dv, i, ((2, down, down_hbm),))
    for store in stores:
        store.wait()


def body(inputs, out_grad, gate_weight, up_weight, down_weight):
    feats, ff = gate_weight.shape
    blocks = (CHUNKS, 4, 16)
    anywhere = pl.BlockSpec(memory_space=pltpu.HBM)
    slot = (CHUNKS, 16, 3 * ff)
    dma = pltpu.SemaphoreType.DMA
    own, other, x_all, d_all, hidden, gate_up_grad = pl.pallas_call(
        comm_kernel,
        out_shape=[
            jax.ShapeDtypeStruct((16, feats), F32),
            jax.ShapeDtypeStruct((2, 16, feats), F32),
            jax.ShapeDtypeStruct((CHUNKS, 2, 2, 16, feats), BF16),
            jax.ShapeDtypeStruct((CHUNKS, 2, 2, 16, feats), BF16),
            jax.ShapeDtypeStruct(blocks + (ff,), BF16),
            jax.ShapeDtypeStruct(blocks + (2 * ff,), BF16),
        ],
        in_specs=[anywhere] * 5,
        out_specs=[pl.BlockSpec(memory_space=pltpu.VMEM)] * 2 + [anywhere] * 4,
        scratch_shapes=[
            pltpu.VMEM((CHUNKS, 2, 2, 2, 16, feats), BF16),
            pltpu.VMEM((feats, ff), BF16),
            pltpu.VMEM((feats, ff), BF16),
            pltpu.VMEM((ff, feats), BF16),
            pltpu.VMEM((CHUNKS, 4, 16, 3 * ff), F32),
            pltpu.VMEM(slot, BF16),
            pltpu.VMEM(slot, BF16),
            pltpu.VMEM(slot, BF16),
            pltpu.VMEM(slot, BF16),
            pltpu.VMEM(slot, BF16),
            pltpu.VMEM(slot, BF16),
            pltpu.VMEM(slot, BF16),
            pltpu.VMEM(slot, BF16),
            pltpu.VMEM(blocks + (3 * ff,), BF16),
            pltpu.VMEM((CHUNKS, 2, 2, 16, feats), F32),
            pltpu.VMEM((CHUNKS, 2, 16, feats), F32),
            pltpu.VMEM((6, 2, 16, feats), F32),
            pltpu.VMEM((6, 2, 16, feats), F32),
            pltpu.VMEM((16, feats), F32),
            pltpu.VMEM((16, feats), F32),
            dma((5,)),
            dma((CHUNKS, PER_CHUNK)),
            dma((CHUNKS, PER_CHUNK)),
            dma((3,)),
            dma((3,)),
            dma((CHUNKS,)),
            dma((CHUNKS,)),
            dma((8,)),
            dma((8,)),
            dma((CHUNKS,)),
            dma((CHUNKS,)),
            dma((6,)),
            dma((6,)),
            dma(()),
            dma(()),
            dma((CHUNKS, 4)),
            pltpu.SemaphoreType.REGULAR((6,)),
        ],
        compiler_params=pltpu.CompilerParams(
            collective_id=0, has_side_effects=True, vmem_limit_bytes=48 * 2**20
        ),
        name="comm",
    )(*(pltpu.with_memory_space_constraint(a, pltpu.HBM) for a in (inputs, out_grad)), gate_weight, up_weight, down_weight)

    def far(i, col):
        z_lo = col // 8
        target = (z_lo + 2) % 4 if i == 0 else (z_lo + 3 - 2 * (z_lo % 2)) % 4
        return (col, target * 8 + col % 8)

    from_far = [lax.ppermute(other[i], "col", [far(i, col) for col in range(32)]) for i in range(2)]

    def flat(a):
        return a.reshape(-1, a.shape[-1])

    tokens = flat(x_all).shape[0]
    gate_weight_grad, up_weight_grad, down_weight_grad = pl.pallas_call(
        weight_grad_kernel,
        out_shape=[
            jax.ShapeDtypeStruct((feats, ff), BF16),
            jax.ShapeDtypeStruct((feats, ff), BF16),
            jax.ShapeDtypeStruct((ff, feats), BF16),
        ],
        in_specs=[pl.BlockSpec(memory_space=pltpu.VMEM)] * 4,
        out_specs=[anywhere] * 3,
        scratch_shapes=[
            pltpu.VMEM((feats, ff), BF16),
            pltpu.VMEM((feats, ff), BF16),
            pltpu.VMEM((ff, feats), BF16),
            dma((3, 4)),
        ],
        compiler_params=pltpu.CompilerParams(vmem_limit_bytes=32 * 2**20),
        cost_estimate=pl.CostEstimate(
            flops=6 * tokens * feats * ff,
            bytes_accessed=6 * feats * ff + 2 * tokens * (2 * feats + 3 * ff),
            transcendentals=0,
        ),
        name="weight_grads",
    )(flat(x_all), flat(d_all), flat(hidden), flat(gate_up_grad))
    input_grad = (own + from_far[0] + from_far[1]).astype(BF16)
    return input_grad, gate_weight_grad, up_weight_grad, down_weight_grad


def solution(mesh):
    return jax.shard_map(
        body,
        mesh=mesh,
        in_specs=(P("col", "row"), P("col", "row"), P("row", "col"), P("row", "col"), P("col", "row")),
        out_specs=(P("col", "row"), P("row", "col"), P("row", "col"), P("col", "row")),
        check_vma=False,
    )
```
